1024 devices in a mesh: seq: 128 (over x, z), tp: 4 (over y), dp: 2 (over core).
Axes of the slice: x: 4, y: 4, z: 32, core: 2. Of those that a mesh axis runs over, the one named last changes fastest.
Arguments:
- frames: bfloat16 [65536, 1536], P(('seq', 'dp')), may hold values from -6 to 6
- lengths: int32 [4], replicated, may hold values from 1 to 32768, 65536 in all
- norm_gain: float32 [1536], replicated, may hold values from 0.25 to 1.75
- qkv_weight: bfloat16 [1536, 3, 1536], P(None, None, 'tp'), may hold values from -0.15625 to 0.15625
- out_weight: bfloat16 [1536, 1536], P('tp'), may hold values from -0.15625 to 0.15625
- conv_gain: float32 [1536], replicated, may hold values from 0.25 to 1.75
- glu_weight: bfloat16 [1536, 2, 1536], P(None, None, 'tp'), may hold values from -0.15625 to 0.15625
- conv_taps: float32 [31, 1536], P(None, 'tp'), may hold values from -1 to 1
- point_weight: bfloat16 [1536, 1536], P('tp'), may hold values from -0.15625 to 0.15625
Outputs:
- layer_out: bfloat16 [65536, 1536], P(('seq', 'dp'), 'tp')
The draws below stay inside these ranges and needn't reach their ends.
Inputs may be any that keep to these rules, and one draw needn't show every extreme that they name: The lengths of the utterances packed in order into the stream; they sum to 65536 and the longest is exactly 32768.
All inputs are finite; a program needn't handle non-finite values.
Results may differ from the reference program's by a relative error of at most 0.012.
Values may be sent and summed in bfloat16 or wider, within the bound.
No kernel may reach another device: no remote copies, remote signals or barrier semaphores. Data moves between devices by JAX's collectives and lax.ppermute only.
A program may use at most 64 MiB of HBM per device.

```python
import math
import jax
import jax.numpy as jnp
import numpy as np
from jax import lax

D = 1536
HEADS = 16
HEAD = 96
KERNEL = 31
FRAMES_DEV = 256
COUNT = 4
FRAMES = 65536
N_TP = 4


def shard_levels(stream_key, extent, split, smallest, top_value):
    level, own = 1.0, jax.random.fold_in(stream_key, 6)
    for axis_at, blocks in split:
        draws = jnp.exp(jax.random.uniform(jax.random.fold_in(own, axis_at), (blocks,), jnp.float32, smallest / len(split), top_value / len(split)))
        level = level * jnp.repeat(draws, extent[axis_at] // blocks).reshape([-1 if axis == axis_at else 1 for axis in range(len(extent))])
    return level


def profile(count, total, most, slope):
    weights = [(1 << 20) // math.isqrt(grade ** slope) + 1 for grade in range(2, count + 1)]
    surplus, counts = total - most - (count - 1), [1] * (count - 1)
    while surplus > 0:
        free = [i for i in range(count - 1) if counts[i] < most]
        pool, left = sum([weights[i] for i in free]), surplus
        for i in free:
            extra = min(most - counts[i], max(1, left * weights[i] // pool), surplus)
            counts[i] = counts[i] + extra
            surplus = surplus - extra
    return np.array([most] + counts)


def ragged(stream_key, number_of, total, bound, lean):
    if number_of == 2:
        one = jax.random.randint(stream_key, (), max(1, total - bound), min(bound, total - 1) + 1)
        return jnp.stack([one, total - one])
    tallies = jnp.asarray(profile(number_of, total, bound, lean), jnp.int32)
    twos = (number_of - 1) // 2
    giver, sink = tallies[1:1 + 2 * twos:2], tallies[2:2 + 2 * twos:2]
    room = jnp.minimum(giver - 1, bound - sink)
    moved = jax.random.randint(jax.random.fold_in(stream_key, 1), (twos,), 0, 1 << 20) % (room + 1)
    tallies = tallies.at[1:1 + 2 * twos:2].set(giver - moved).at[2:2 + 2 * twos:2].set(sink + moved)
    return tallies[jax.random.permutation(jax.random.fold_in(stream_key, 2), number_of)]


def scatter_about(rng, shape, width, reach, split=(), kind=jnp.bfloat16):
    level = shard_levels(rng, shape, split, -0.22, 0.18) if split else 1.0
    array = jax.random.normal(rng, shape, jnp.float32) * width * level
    return jnp.minimum(jnp.maximum(array, -reach), reach).astype(kind)


def setup_inputs(seed: int = 0) -> dict:
    arg_keys = jax.random.split(jax.random.key(seed), 10)
    frames = scatter_about(arg_keys[0], (FRAMES, D), 1.0, 6.0, ((0, 256),))
    lengths = ragged(arg_keys[1], COUNT, FRAMES, FRAMES // 2, 2).astype(jnp.int32)
    norm_gain = jnp.clip(1.0 + 0.15 * jax.random.normal(arg_keys[2], (D,), jnp.float32), 0.25, 1.75)
    qkv_weight = scatter_about(arg_keys[3], (D, 3, HEADS * HEAD), D ** -0.5, 0.15625, ((2, 4),))
    out_weight = scatter_about(arg_keys[4], (HEADS * HEAD, D), (HEADS * HEAD) ** -0.5, 0.15625, ((0, 4),))
    conv_gain = jnp.clip(1.0 + 0.15 * jax.random.normal(arg_keys[5], (D,), jnp.float32), 0.25, 1.75)
    glu_weight = scatter_about(arg_keys[6], (D, 2, D), D ** -0.5, 0.15625, ((2, 4),))
    conv_taps = scatter_about(arg_keys[7], (KERNEL, D), KERNEL ** -0.5, 1.0, ((1, 4),), jnp.float32)
    point_weight = scatter_about(arg_keys[8], (D, D), D ** -0.5, 0.15625, ((0, 4),))
    return dict(frames=frames, lengths=lengths, norm_gain=norm_gain, qkv_weight=qkv_weight, out_weight=out_weight, conv_gain=conv_gain, glu_weight=glu_weight, conv_taps=conv_taps, point_weight=point_weight)


EPSILON = 1e-05

def layer_norm(values, gain):
    values = values.astype(jnp.float32)
    centre_mean = lax.optimization_barrier(jnp.mean(values, axis=-1, keepdims=True))
    centred = values - centre_mean
    variance = lax.optimization_barrier(jnp.mean(centred * centred, axis=-1, keepdims=True))
    return centred * lax.rsqrt(variance + EPSILON) * gain

def utterance_ids(lengths, first_frame, frame_count, frame_total):
    utter_ends = jnp.cumsum(lengths).astype(jnp.int32)
    positions = (first_frame + jnp.arange(frame_count, dtype=jnp.int32)).astype(jnp.int32)
    found = lax.optimization_barrier(jnp.sum((positions[:, None] >= utter_ends[None, :]).astype(jnp.int32), axis=1)).astype(jnp.int32)
    outside = jnp.where(positions < 0, -1, -2).astype(jnp.int32)
    inside = (positions >= 0) & (positions < frame_total)
    return jnp.where(inside, found, outside).astype(jnp.int32)

def attend_rows(query_rows, key_rows, value_rows, query_ids, key_ids):
    query_heads = query_rows.astype(jnp.float32).reshape(query_rows.shape[0], -1, HEAD)
    key_heads = key_rows.astype(jnp.float32).reshape(key_rows.shape[0], -1, HEAD)
    value_heads = value_rows.astype(jnp.float32).reshape(value_rows.shape[0], -1, HEAD)
    scores = jnp.einsum('qhd,khd->hqk', query_heads, key_heads) * HEAD ** (-0.5)
    same_utter = (query_ids[:, None] == key_ids[None, :])[None]
    weights = jnp.where(same_utter, jnp.exp(scores), 0.0)
    probs = (weights / lax.optimization_barrier(jnp.sum(weights, axis=-1, keepdims=True))).astype(jnp.bfloat16)
    mixed_rows = jnp.einsum('hqk,khd->qhd', probs.astype(jnp.float32), value_heads)
    return mixed_rows.reshape(query_rows.shape[0], -1).astype(jnp.bfloat16)

def depthwise(window, conv_ids, conv_taps, frame_rows, margin):
    window = window.astype(jnp.float32)
    centre_ids = conv_ids[margin:margin + frame_rows]
    running = jnp.zeros((frame_rows, window.shape[1]), jnp.float32)
    for tap_index in range(conv_taps.shape[0]):
        keep_mask = (conv_ids[tap_index:tap_index + frame_rows] == centre_ids)[:, None]
        running = running + jnp.where(keep_mask, window[tap_index:tap_index + frame_rows] * conv_taps[tap_index], 0.0)
    return (running * jax.nn.sigmoid(running)).astype(jnp.bfloat16)

def add_terms(running, left, right, group_cols):
    for tp_part in range(N_TP):
        lower = tp_part * group_cols
        piece = jnp.dot(left[:, lower:lower + group_cols], right[lower:lower + group_cols], preferred_element_type=jnp.float32).astype(jnp.bfloat16)
        piece = lax.optimization_barrier(piece)
        running = running + piece.astype(jnp.float32)
    return running

def reference(frames, lengths, norm_gain, qkv_weight, out_weight, conv_gain, glu_weight, conv_taps, point_weight):
    block_count = FRAMES // FRAMES_DEV
    inner = HEADS * HEAD
    margin = KERNEL // 2
    blocks = frames.reshape(block_count, FRAMES_DEV, D)
    block_list = jnp.arange(block_count, dtype=jnp.int32)
    flat_qkv = qkv_weight.reshape(D, 3 * inner)

    def project(block):
        normed = layer_norm(block, norm_gain).astype(jnp.bfloat16)
        return jnp.dot(normed, flat_qkv, preferred_element_type=jnp.float32).astype(jnp.bfloat16)
    packed = lax.map(project, blocks)
    empty_block = jnp.zeros((1, FRAMES_DEV, 3 * inner), jnp.bfloat16)
    padded = jnp.concatenate([empty_block, packed, empty_block], axis=0)

    def attend_block(block_index):
        own_rows = lax.dynamic_index_in_dim(packed, block_index, 0, keepdims=False)
        nearby = lax.dynamic_slice_in_dim(padded, block_index, 3, 0).reshape(3 * FRAMES_DEV, 3 * inner)
        window_ids = utterance_ids(lengths, block_index * FRAMES_DEV - FRAMES_DEV, 3 * FRAMES_DEV, FRAMES)
        return attend_rows(own_rows[:, :inner], nearby[:, inner:2 * inner], nearby[:, 2 * inner:], window_ids[FRAMES_DEV:2 * FRAMES_DEV], window_ids)
    mixed = lax.map(attend_block, block_list)

    def residual_block(pair):
        block, mixed_rows = pair
        return add_terms(block.astype(jnp.float32), mixed_rows, out_weight, inner // N_TP)
    residual = lax.map(residual_block, (blocks, mixed))
    flat_glu = glu_weight.reshape(D, 2 * D)

    def glu_block(rows_in):
        normed = layer_norm(rows_in, conv_gain).astype(jnp.bfloat16)
        glu_out = jnp.dot(normed, flat_glu, preferred_element_type=jnp.float32)
        return (glu_out[:, :D] * jax.nn.sigmoid(glu_out[:, D:])).astype(jnp.bfloat16)
    gated = lax.map(glu_block, residual)
    empty_rows = jnp.zeros((FRAMES_DEV, D), jnp.bfloat16)
    flat_gated = jnp.concatenate([empty_rows, gated.reshape(FRAMES, D), empty_rows], axis=0)

    def conv_block(pair):
        block_index, rows_in = pair
        window = lax.dynamic_slice_in_dim(flat_gated, block_index * FRAMES_DEV + FRAMES_DEV - margin, FRAMES_DEV + 2 * margin, 0)
        conv_ids = utterance_ids(lengths, block_index * FRAMES_DEV - margin, FRAMES_DEV + 2 * margin, FRAMES)
        activated = depthwise(window, conv_ids, conv_taps, FRAMES_DEV, margin)
        return add_terms(rows_in, activated, point_weight, D // N_TP).astype(jnp.bfloat16)
    layer_out = lax.map(conv_block, (block_list, residual))
    return layer_out.reshape(FRAMES, D)
```

```python
import jax
import jax.numpy as jnp
from jax import lax
from jax.experimental import pallas as pl
from jax.experimental.pallas import tpu as pltpu
from jax.sharding import PartitionSpec as P

HEAD = 96
KERNEL = 31
MARGIN = KERNEL // 2
HALO = 16
LANES = 128
EPSILON = 1e-05
LOG2E = 1.4426950408889634

VMEM = pl.BlockSpec(memory_space=pltpu.VMEM)
SMEM = pl.BlockSpec(memory_space=pltpu.SMEM)


def params():
    return pltpu.CompilerParams(vmem_limit_bytes=48 * 1024 * 1024)


def cost(flops, size, transcendentals=0):
    return pl.CostEstimate(flops=flops, bytes_accessed=size, transcendentals=transcendentals)


def along_stream(x, step):
    axes = ("seq", "dp")
    devices = lax.axis_size(axes)
    pairs = [(i, i + step) for i in range(devices) if 0 <= i + step < devices]
    return lax.ppermute(x, axes, pairs)


def matmul(left, right):
    return jnp.dot(left, right, preferred_element_type=jnp.float32)


def first_row(rows):
    return (lax.axis_index("seq") * lax.axis_size("dp") + lax.axis_index("dp")) * rows


def ends_of(lengths_ref):
    ends, total = [], jnp.int32(0)
    for i in range(lengths_ref.shape[0]):
        total = total + lengths_ref[i]
        ends.append(total)
    return ends


def ids_of(positions, ends):
    found = jnp.zeros_like(positions)
    for end in ends:
        found = found + (positions >= end).astype(jnp.int32)
    return jnp.where(positions < 0, -1, found)


def project_kernel(frames_ref, gain_ref, weight_ref, normed_ref, out_ref):
    @pl.when(pl.program_id(0) == 0)
    def _():
        values = frames_ref[...].astype(jnp.float32)
        centred = values - jnp.mean(values, axis=-1, keepdims=True)
        variance = jnp.mean(centred * centred, axis=-1, keepdims=True)
        normed_ref[...] = (centred * lax.rsqrt(variance + EPSILON) * gain_ref[...]).astype(jnp.bfloat16)

    out_ref[...] = matmul(normed_ref[...], weight_ref[0]).astype(jnp.bfloat16)


def query_kernel(normed_ref, weight_ref, out_ref):
    out_ref[...] = matmul(normed_ref[...], weight_ref[0]).astype(jnp.bfloat16)


def attend_kernel(lengths_ref, query_ref, before_ref, own_ref, after_ref, weight_ref, out_ref):
    rows, cols = query_ref.shape
    heads = cols // HEAD
    start = first_row(rows)
    ends = ends_of(lengths_ref)
    query_ids = ids_of(start + lax.broadcasted_iota(jnp.int32, (rows, 1), 0), ends)
    sides = (before_ref, own_ref, after_ref)
    same = []
    for side in range(3):
        at = start + (side - 1) * rows
        same.append(query_ids == ids_of(at + lax.broadcasted_iota(jnp.int32, (1, rows), 1), ends))
    scale = HEAD ** (-0.5) * LOG2E
    lane_groups = [None] * (cols // LANES)
    for head in range(heads):
        low, high = head * HEAD, (head + 1) * HEAD
        left, right = low // LANES * LANES, -(-high // LANES) * LANES
        lane = left + lax.broadcasted_iota(jnp.int32, (1, right - left), 1)
        mine = (lane >= low) & (lane < high)
        query = jnp.where(mine, query_ref[:, left:right], jnp.zeros((), jnp.bfloat16))
        weights, total = [], None
        for side in range(3):
            scores = lax.dot_general(
                query,
                sides[side][:, left:right],
                (((1,), (1,)), ((), ())),
                preferred_element_type=jnp.float32,
            )
            piece = jnp.where(same[side], jnp.exp2(scores * scale), 0.0)
            weights.append(piece)
            part = jnp.sum(piece, axis=-1, keepdims=True)
            total = part if total is None else total + part
        shift = jnp.where(total > 1.0, 2.0**-20, 2.0**20)
        inverse = 1.0 / (total * shift)
        mixed = None
        for side in range(3):
            probs = (weights[side] * inverse * shift).astype(jnp.bfloat16)
            term = matmul(probs, sides[side][:, cols + left : cols + right])
            mixed = term if mixed is None else mixed + term
        for group in range(left // LANES, right // LANES):
            lanes = slice(group * LANES - left, (group + 1) * LANES - left)
            old, new = lane_groups[group], mixed[:, lanes]
            lane_groups[group] = new if old is None else jnp.where(mine[:, lanes], new, old)
    mixed_rows = jnp.concatenate([x.astype(jnp.bfloat16) for x in lane_groups], axis=1)
    chunks, _, width = out_ref.shape
    for chunk in range(chunks):
        part = matmul(mixed_rows, weight_ref[:, chunk * width : (chunk + 1) * width])
        out_ref[chunk] = part.astype(jnp.bfloat16)


def glu_kernel(residual_ref, gain_ref, weight_ref, out_ref):
    chunks, _, width = residual_ref.shape
    model_width = chunks * width
    parts = [residual_ref[i].astype(jnp.float32) for i in range(chunks)]
    mean = sum(jnp.sum(x, axis=-1, keepdims=True) for x in parts) / model_width
    parts = [x - mean for x in parts]
    variance = sum(jnp.sum(x * x, axis=-1, keepdims=True) for x in parts) / model_width
    inverse = lax.rsqrt(variance + EPSILON)
    value = gate = None
    for i in range(chunks):
        span = slice(i * width, (i + 1) * width)
        normed = (parts[i] * inverse * gain_ref[:, span]).astype(jnp.bfloat16)
        value_term = matmul(normed, weight_ref[0, span])
        gate_term = matmul(normed, weight_ref[1, span])
        value = value_term if value is None else value + value_term
        gate = gate_term if gate is None else gate + gate_term
    out_ref[...] = (value * jax.nn.sigmoid(gate)).astype(jnp.bfloat16)


def conv_kernel(lengths_ref, before_ref, own_ref, after_ref, taps_ref, weight_ref, out_ref, window_ref):
    rows, cols = own_ref.shape
    start = first_row(rows)
    ends = ends_of(lengths_ref)
    positions = start + lax.broadcasted_iota(jnp.int32, (rows, LANES), 0)
    first = jnp.zeros_like(positions)
    last = jnp.zeros_like(positions)
    begin = jnp.int32(0)
    for end in ends:
        inside = (positions >= begin) & (positions < end)
        first = jnp.where(inside, begin - positions, first)
        last = jnp.where(inside, end - 1 - positions, last)
        begin = end
    window_ref[:HALO] = before_ref[...].astype(jnp.float32)
    window_ref[HALO : HALO + rows] = own_ref[...].astype(jnp.float32)
    window_ref[HALO + rows :] = after_ref[...].astype(jnp.float32)
    step = 64
    activated = []
    for row in range(0, rows, step):
        groups = []
        low, high = first[row : row + step], last[row : row + step]
        for lane in range(0, cols, LANES):
            running = jnp.zeros((step, LANES), jnp.float32)
            for tap in range(KERNEL):
                offset = tap - MARGIN
                at = HALO + offset + row
                term = window_ref[at : at + step, lane : lane + LANES] * taps_ref[tap : tap + 1, lane : lane + LANES]
                if offset:
                    keep = (low <= offset) if offset < 0 else (high >= offset)
                    term = jnp.where(keep, term, 0.0)
                running = running + term
            groups.append((running * jax.nn.sigmoid(running)).astype(jnp.bfloat16))
        activated.append(jnp.concatenate(groups, axis=1))
    activated = jnp.concatenate(activated, axis=0)
    chunks, _, width = out_ref.shape
    for chunk in range(chunks):
        part = matmul(activated, weight_ref[:, chunk * width : (chunk + 1) * width])
        out_ref[chunk] = part.astype(jnp.bfloat16)


def body(
    frames,
    lengths,
    norm_gain,
    qkv_weight,
    out_weight,
    conv_gain,
    glu_weight,
    conv_taps,
    point_weight,
):
    rows, model_width = frames.shape
    group_cols = qkv_weight.shape[2]
    chan_cols = glu_weight.shape[2]
    parts = lax.axis_size("tp")
    out_cols = model_width // parts
    bf16 = jnp.bfloat16
    qkv = jnp.swapaxes(qkv_weight, 0, 1)

    normed, keys_values = pl.pallas_call(
        project_kernel,
        grid=(2,),
        in_specs=[
            pl.BlockSpec((rows, model_width), lambda i: (0, 0)),
            pl.BlockSpec((1, model_width), lambda i: (0, 0)),
            pl.BlockSpec((1, model_width, group_cols), lambda i: (i + 1, 0, 0)),
        ],
        out_specs=[
            pl.BlockSpec((rows, model_width), lambda i: (0, 0)),
            pl.BlockSpec((rows, group_cols), lambda i: (0, i)),
        ],
        out_shape=[
            jax.ShapeDtypeStruct((rows, model_width), bf16),
            jax.ShapeDtypeStruct((rows, 2 * group_cols), bf16),
        ],
        compiler_params=params(),
        cost_estimate=cost(4 * rows * model_width * group_cols, 4_000_000),
        name="project",
    )(frames, norm_gain[None], qkv)
    before = along_stream(keys_values, 1)
    after = along_stream(keys_values, -1)
    query = pl.pallas_call(
        query_kernel,
        grid=(1,),
        in_specs=[
            pl.BlockSpec((rows, model_width), lambda i: (0, 0)),
            pl.BlockSpec((1, model_width, group_cols), lambda i: (0, 0, 0)),
        ],
        out_specs=pl.BlockSpec((rows, group_cols), lambda i: (0, 0)),
        out_shape=jax.ShapeDtypeStruct((rows, group_cols), bf16),
        compiler_params=params(),
        cost_estimate=cost(2 * rows * model_width * group_cols, 2_200_000),
        name="query",
    )(normed, qkv)
    attn_terms = pl.pallas_call(
        attend_kernel,
        in_specs=[SMEM] + [VMEM] * 5,
        out_specs=VMEM,
        out_shape=jax.ShapeDtypeStruct((parts, rows, out_cols), bf16),
        compiler_params=params(),
        cost_estimate=cost(10**9, 4_000_000, 4 * 3 * rows * rows),
        name="attend",
    )(lengths, query, before, keys_values, after, out_weight)
    attn_terms = lax.all_to_all(attn_terms, "tp", 0, 0, tiled=True)
    own_frames = lax.dynamic_slice_in_dim(frames, lax.axis_index("tp") * out_cols, out_cols, 1)
    residual = own_frames.astype(jnp.float32) + jnp.sum(attn_terms.astype(jnp.float32), axis=0)
    gathered = lax.all_gather(residual.astype(bf16), "tp", axis=0)
    gated = pl.pallas_call(
        glu_kernel,
        in_specs=[VMEM] * 3,
        out_specs=VMEM,
        out_shape=jax.ShapeDtypeStruct((rows, chan_cols), bf16),
        compiler_params=params(),
        cost_estimate=cost(4 * rows * model_width * chan_cols, 3_500_000),
        name="glu",
    )(gathered, conv_gain[None], jnp.swapaxes(glu_weight, 0, 1))
    conv_before = along_stream(gated[rows - HALO :], 1)
    conv_after = along_stream(gated[:HALO], -1)
    conv_terms = pl.pallas_call(
        conv_kernel,
        in_specs=[SMEM] + [VMEM] * 5,
        out_specs=VMEM,
        out_shape=jax.ShapeDtypeStruct((parts, rows, out_cols), bf16),
        scratch_shapes=[pltpu.VMEM((rows + 2 * HALO, chan_cols), jnp.float32)],
        compiler_params=params(),
        cost_estimate=cost(2 * rows * model_width * chan_cols, 2_500_000),
        name="conv",
    )(lengths, conv_before, gated, conv_after, conv_taps, point_weight)
    conv_terms = lax.all_to_all(conv_terms, "tp", 0, 0, tiled=True)
    return (residual + jnp.sum(conv_terms.astype(jnp.float32), axis=0)).astype(bf16)


def solution(mesh):
    return jax.shard_map(
        body,
        mesh=mesh,
        in_specs=(
            P(("seq", "dp"), None),
            P(),
            P(),
            P(None, None, "tp"),
            P("tp", None),
            P(),
            P(None, None, "tp"),
            P(None, "tp"),
            P("tp", None),
        ),
        out_specs=P(("seq", "dp"), "tp"),
        check_vma=False,
    )
```

```python
import jax
import jax.numpy as jnp
from jax import lax
from jax.experimental import pallas as pl
from jax.experimental.pallas import tpu as pltpu
from jax.sharding import PartitionSpec as P

HEAD = 96
KERNEL = 31
MARGIN = KERNEL // 2
HALO = 16
LANES = 128
EPSILON = 1e-05
LOG2E = 1.4426950408889634
MASKED = -1e38

VMEM = pl.BlockSpec(memory_space=pltpu.VMEM)
HBM = pl.BlockSpec(memory_space=pltpu.HBM)
SMEM = pl.BlockSpec(memory_space=pltpu.SMEM)


def params(mebibytes=48):
    return pltpu.CompilerParams(vmem_limit_bytes=mebibytes * 1024 * 1024)


def cost(flops, size, transcendentals=0):
    return pl.CostEstimate(flops=flops, bytes_accessed=size, transcendentals=transcendentals)


def swap_between_chips(x):
    axes = ("seq", "dp")
    pairs = [(i, i + 1) for i in range(1, lax.axis_size(axes) - 1, 2)]
    return lax.ppermute(x, axes, pairs + [(j, i) for i, j in pairs])


def swap_within_chip(x):
    return lax.ppermute(x, "dp", [(0, 1), (1, 0)])


def matmul(left, right):
    return jnp.dot(left, right, preferred_element_type=jnp.float32)


def first_row(rows):
    return (lax.axis_index("seq") * lax.axis_size("dp") + lax.axis_index("dp")) * rows


def ends_of(lengths_ref):
    ends, total = [], jnp.int32(0)
    for i in range(lengths_ref.shape[0]):
        total = total + lengths_ref[i]
        ends.append(total)
    return ends


def ids_of(positions, ends):
    found = jnp.zeros_like(positions)
    for end in ends:
        found = found + (positions >= end).astype(jnp.int32)
    return jnp.where(positions < 0, -1, found)


def project_kernel(frames_hbm, gain_ref, weight_hbm, normed_ref, out_ref, frames_buf, weight_buf, sems):
    rows, model_width = frames_buf.shape
    cols = weight_buf.shape[2]
    half = rows // 2
    copies = []
    for i in range(2):
        span = pl.ds(i * half, half)
        copies.append(pltpu.make_async_copy(frames_hbm.at[span], frames_buf.at[span], sems.at[i]))
    for i in range(2):
        copies.append(pltpu.make_async_copy(weight_hbm.at[i + 1], weight_buf.at[i], sems.at[i + 2]))
    for copy in copies:
        copy.start()
    for i in range(2):
        copies[i].wait()
        span = slice(i * half, (i + 1) * half)
        values = frames_buf[span].astype(jnp.float32)
        centred = values - jnp.mean(values, axis=-1, keepdims=True)
        inverse = lax.rsqrt(jnp.mean(centred * centred, axis=-1, keepdims=True) + EPSILON)
        for j in range(model_width // LANES):
            lanes = slice(j * LANES, (j + 1) * LANES)
            normed_ref[span, lanes] = (centred[:, lanes] * inverse * gain_ref[j : j + 1]).astype(jnp.bfloat16)
    for i in range(2):
        copies[i + 2].wait()
        out_ref[:, i * cols : (i + 1) * cols] = matmul(normed_ref[...], weight_buf[i]).astype(jnp.bfloat16)


def head_window(head):
    low, high = head * HEAD, (head + 1) * HEAD
    left, right = low // LANES * LANES, -(-high // LANES) * LANES
    lane = left + lax.broadcasted_iota(jnp.int32, (1, right - left), 1)
    return left, right, (lane >= low) & (lane < high)


def scores_of(query, side_ref, left, right, same):
    scores = lax.dot_general(
        query, side_ref[:, left:right], (((1,), (1,)), ((), ())), preferred_element_type=jnp.float32
    )
    return jnp.where(same, scores * (HEAD ** (-0.5) * LOG2E), MASKED)


def place(groups, left, right, mine, rows_value):
    for group in range(left // LANES, right // LANES):
        lanes = slice(group * LANES - left, (group + 1) * LANES - left)
        old, new = groups[group], rows_value[:, lanes]
        groups[group] = new if old is None else jnp.where(mine[:, lanes], new, old)


def own_kernel(lengths_ref, normed_ref, weight_hbm, own_ref, query_ref, mixed_ref, top_ref, total_ref, weight_buf, sem):
    copy = pltpu.make_async_copy(weight_hbm.at[0], weight_buf, sem.at[0])
    copy.start()
    rows, cols = query_ref.shape
    heads = cols // HEAD
    start = first_row(rows)
    ends = ends_of(lengths_ref)
    query_ids = ids_of(start + lax.broadcasted_iota(jnp.int32, (rows, 1), 0), ends)
    same = query_ids == ids_of(start + lax.broadcasted_iota(jnp.int32, (1, rows), 1), ends)
    lane = lax.broadcasted_iota(jnp.int32, (rows, LANES), 1)
    tops = totals = jnp.zeros((rows, LANES), jnp.float32)
    copy.wait()
    queries = matmul(normed_ref[...], weight_buf[...]).astype(jnp.bfloat16)
    query_ref[...] = queries
    groups = [None] * (cols // LANES)
    for head in range(heads):
        left, right, mine = head_window(head)
        query = jnp.where(mine, queries[:, left:right], jnp.zeros((), jnp.bfloat16))
        scores = scores_of(query, own_ref, left, right, same)
        top = jnp.max(scores, axis=-1, keepdims=True)
        weights = jnp.exp2(scores - top)
        tops = jnp.where(lane == head, top, tops)
        totals = jnp.where(lane == head, jnp.sum(weights, axis=-1, keepdims=True), totals)
        place(groups, left, right, mine, matmul(weights.astype(jnp.bfloat16), own_ref[:, cols + left : cols + right]))
    for group, value in enumerate(groups):
        mixed_ref[:, group * LANES : (group + 1) * LANES] = value
    top_ref[...] = tops
    total_ref[...] = totals


def attend_kernel(
    lengths_ref, query_ref, mixed_ref, top_ref, total_ref, inner_ref, outer_ref, weight_ref, out_ref
):
    rows, cols = query_ref.shape
    heads = cols // HEAD
    start = first_row(rows)
    ends = ends_of(lengths_ref)
    query_ids = ids_of(start + lax.broadcasted_iota(jnp.int32, (rows, 1), 0), ends)
    outward = 2 * lax.axis_index("dp") - 1
    same = []
    for step in (outward, -outward):
        at = start + step * rows
        same.append(query_ids == ids_of(at + lax.broadcasted_iota(jnp.int32, (1, rows), 1), ends))
    groups = [None] * (cols // LANES)
    for head in range(heads):
        left, right, mine = head_window(head)
        query = jnp.where(mine, query_ref[:, left:right], jnp.zeros((), jnp.bfloat16))
        outer = scores_of(query, outer_ref, left, right, same[0])
        inner = scores_of(query, inner_ref, left, right, same[1])
        old_top = top_ref[:, head : head + 1]
        top = jnp.maximum(old_top, jnp.max(jnp.maximum(outer, inner), axis=-1, keepdims=True))
        outer, inner = jnp.exp2(outer - top), jnp.exp2(inner - top)
        fade = jnp.exp2(old_top - top)
        total = total_ref[:, head : head + 1] * fade + jnp.sum(outer + inner, axis=-1, keepdims=True)
        mixed = mixed_ref[:, left:right] * fade
        mixed = mixed + matmul(outer.astype(jnp.bfloat16), outer_ref[:, cols + left : cols + right])
        mixed = mixed + matmul(inner.astype(jnp.bfloat16), inner_ref[:, cols + left : cols + right])
        place(groups, left, right, mine, mixed * (1.0 / total))
    mixed_rows = jnp.concatenate([x.astype(jnp.bfloat16) for x in groups], axis=1)
    chunks, _, width = out_ref.shape
    for chunk in range(chunks):
        part = matmul(mixed_rows, weight_ref[:, chunk * width : (chunk + 1) * width])
        out_ref[chunk] = part.astype(jnp.bfloat16)


def glu_kernel(residual_ref, gain_ref, weight_ref, out_ref, outer_ref, inner_ref):
    chunks, rows, width = residual_ref.shape
    model_width = chunks * width
    parts = [residual_ref[i].astype(jnp.float32) for i in range(chunks)]
    mean = sum(jnp.sum(x, axis=-1, keepdims=True) for x in parts) / model_width
    parts = [x - mean for x in parts]
    variance = sum(jnp.sum(x * x, axis=-1, keepdims=True) for x in parts) / model_width
    inverse = lax.rsqrt(variance + EPSILON)
    value = gate = None
    for i in range(chunks):
        normed = []
        for j in range(width // LANES):
            at = i * (width // LANES) + j
            lanes = slice(j * LANES, (j + 1) * LANES)
            normed.append((parts[i][:, lanes] * inverse * gain_ref[at : at + 1]).astype(jnp.bfloat16))
        normed = jnp.concatenate(normed, axis=1)
        span = slice(i * width, (i + 1) * width)
        value_term = matmul(normed, weight_ref[0, span])
        gate_term = matmul(normed, weight_ref[1, span])
        value = value_term if value is None else value + value_term
        gate = gate_term if gate is None else gate + gate_term
    gated = (value * jax.nn.sigmoid(gate)).astype(jnp.bfloat16)
    out_ref[...] = gated
    even = lax.axis_index("dp") == 0
    outer_ref[...] = jnp.where(even, gated[:HALO], gated[rows - HALO :])
    inner_ref[...] = jnp.where(even, gated[rows - HALO :], gated[:HALO])


def spans_of(start, count, ends):
    positions = start + lax.broadcasted_iota(jnp.int32, (count, LANES), 0)
    first = jnp.zeros_like(positions)
    last = jnp.zeros_like(positions)
    begin = jnp.int32(0)
    for end in ends:
        inside = (positions >= begin) & (positions < end)
        first = jnp.where(inside, begin - positions, first)
        last = jnp.where(inside, end - 1 - positions, last)
        begin = end
    return first, last


def convolve(window_ref, base, first, last, taps_ref):
    count = first.shape[0]
    cols = taps_ref.shape[1]
    running = [jnp.zeros((count, LANES), jnp.float32)] * (cols // LANES)
    for tap in range(KERNEL):
        offset = tap - MARGIN
        at = base + HALO + offset
        keep = None if offset == 0 else (first <= offset) if offset < 0 else (last >= offset)
        for group in range(cols // LANES):
            lanes = slice(group * LANES, (group + 1) * LANES)
            term = window_ref[at : at + count, lanes] * taps_ref[tap : tap + 1, lanes]
            if keep is not None:
                term = jnp.where(keep, term, 0.0)
            running[group] = running[group] + term
    return jnp.concatenate([(x * jax.nn.sigmoid(x)).astype(jnp.bfloat16) for x in running], axis=1)


def inside_kernel(lengths_ref, own_ref, taps_ref, out_ref, window_ref):
    start = first_row(own_ref.shape[0]) + HALO
    ends = ends_of(lengths_ref)
    window_ref[...] = own_ref[...].astype(jnp.float32)
    step = 2 * HALO
    for row in range(0, out_ref.shape[0], step):
        first, last = spans_of(start + row, step, ends)
        out_ref[row : row + step] = convolve(window_ref, row, first, last, taps_ref)


def conv_kernel(
    lengths_ref, outer_ref, inner_ref, own_ref, inside_ref, taps_ref, weight_ref, out_ref, low_ref, high_ref
):
    rows = own_ref.shape[0]
    start = first_row(rows)
    ends = ends_of(lengths_ref)
    even = lax.axis_index("dp") == 0
    low_ref[:HALO] = jnp.where(even, outer_ref[...], inner_ref[...]).astype(jnp.float32)
    low_ref[HALO:] = own_ref[: 2 * HALO].astype(jnp.float32)
    high_ref[: 2 * HALO] = own_ref[rows - 2 * HALO :].astype(jnp.float32)
    high_ref[2 * HALO :] = jnp.where(even, inner_ref[...], outer_ref[...]).astype(jnp.float32)
    low = convolve(low_ref, 0, *spans_of(start, HALO, ends), taps_ref)
    high = convolve(high_ref, 0, *spans_of(start + rows - HALO, HALO, ends), taps_ref)
    activated = jnp.concatenate([low, inside_ref[...], high], axis=0)
    chunks, _, width = out_ref.shape
    for chunk in range(chunks):
        part = matmul(activated, weight_ref[:, chunk * width : (chunk + 1) * width])
        out_ref[chunk] = part.astype(jnp.bfloat16)


def body(
    frames,
    lengths,
    norm_gain,
    qkv_weight,
    out_weight,
    conv_gain,
    glu_weight,
    conv_taps,
    point_weight,
):
    rows, model_width = frames.shape
    group_cols = qkv_weight.shape[2]
    chan_cols = glu_weight.shape[2]
    parts = lax.axis_size("tp")
    out_cols = model_width // parts
    bf16 = jnp.bfloat16
    qkv = jnp.swapaxes(qkv_weight, 0, 1)

    shape = jax.ShapeDtypeStruct

    normed, keys_values = pl.pallas_call(
        project_kernel,
        in_specs=[HBM, VMEM, HBM],
        out_specs=[VMEM, VMEM],
        out_shape=[shape((rows, model_width), bf16), shape((rows, 2 * group_cols), bf16)],
        scratch_shapes=[
            pltpu.VMEM((rows, model_width), bf16),
            pltpu.VMEM((2, model_width, group_cols), bf16),
            pltpu.SemaphoreType.DMA((4,)),
        ],
        compiler_params=params(53),
        cost_estimate=cost(4 * rows * model_width * group_cols, 4_000_000),
        name="project",
    )(frames, norm_gain.reshape(-1, LANES), qkv)
    inner = swap_within_chip(keys_values)
    outer = swap_between_chips(keys_values)
    query, mixed, top, total = pl.pallas_call(
        own_kernel,
        in_specs=[SMEM, VMEM, HBM, VMEM],
        out_specs=[VMEM] * 4,
        out_shape=[
            shape((rows, group_cols), bf16),
            shape((rows, group_cols), jnp.float32),
            shape((rows, LANES), jnp.float32),
            shape((rows, LANES), jnp.float32),
        ],
        scratch_shapes=[pltpu.VMEM((model_width, group_cols), bf16), pltpu.SemaphoreType.DMA((1,))],
        compiler_params=params(52),
        cost_estimate=cost(10**9, 4_000_000, 4 * rows * rows),
        name="own",
    )(lengths, normed, qkv, keys_values)
    attn_terms = pl.pallas_call(
        attend_kernel,
        in_specs=[SMEM] + [VMEM] * 7,
        out_specs=VMEM,
        out_shape=shape((parts, rows, out_cols), bf16),
        compiler_params=params(),
        cost_estimate=cost(10**9, 4_000_000, 8 * rows * rows),
        name="attend",
    )(lengths, query, mixed, top, total, inner, outer, out_weight)
    attn_terms = lax.all_to_all(attn_terms, "tp", 0, 0, tiled=True)
    own_frames = lax.dynamic_slice_in_dim(frames, lax.axis_index("tp") * out_cols, out_cols, 1)
    residual = own_frames.astype(jnp.float32) + jnp.sum(attn_terms.astype(jnp.float32), axis=0)
    gathered = lax.all_gather(residual.astype(bf16), "tp", axis=0)
    gated, outer_rows, inner_rows = pl.pallas_call(
        glu_kernel,
        in_specs=[VMEM] * 3,
        out_specs=[VMEM] * 3,
        out_shape=[shape((rows, chan_cols), bf16)] + [shape((HALO, chan_cols), bf16)] * 2,
        compiler_params=params(),
        cost_estimate=cost(4 * rows * model_width * chan_cols, 3_500_000),
        name="glu",
    )(gathered, conv_gain.reshape(-1, LANES), jnp.swapaxes(glu_weight, 0, 1))
    outer_rows = swap_between_chips(outer_rows)
    inner_rows = swap_within_chip(inner_rows)
    inside = pl.pallas_call(
        inside_kernel,
        in_specs=[SMEM, VMEM, VMEM],
        out_specs=VMEM,
        out_shape=shape((rows - 2 * HALO, chan_cols), bf16),
        scratch_shapes=[pltpu.VMEM((rows, chan_cols), jnp.float32)],
        compiler_params=params(),
        cost_estimate=cost(10**9, 4_000_000),
        name="inside",
    )(lengths, gated, conv_taps)
    conv_terms = pl.pallas_call(
        conv_kernel,
        in_specs=[SMEM] + [VMEM] * 6,
        out_specs=VMEM,
        out_shape=shape((parts, rows, out_cols), bf16),
        scratch_shapes=[pltpu.VMEM((3 * HALO, chan_cols), jnp.float32)] * 2,
        compiler_params=params(),
        cost_estimate=cost(2 * rows * model_width * chan_cols, 2_500_000),
        name="conv",
    )(lengths, outer_rows, inner_rows, gated, inside, conv_taps, point_weight)
    conv_terms = lax.all_to_all(conv_terms, "tp", 0, 0, tiled=True)
    return (residual + jnp.sum(conv_terms.astype(jnp.float32), axis=0)).astype(bf16)


def solution(mesh):
    return jax.shard_map(
        body,
        mesh=mesh,
        in_specs=(
            P(("seq", "dp"), None),
            P(),
            P(),
            P(None, None, "tp"),
            P("tp", None),
            P(),
            P(None, None, "tp"),
            P(None, "tp"),
            P("tp", None),
        ),
        out_specs=P(("seq", "dp"), "tp"),
        check_vma=False,
    )
```

```python
import functools

import jax
import jax.numpy as jnp
from jax import lax
from jax.experimental import pallas as pl
from jax.experimental.pallas import tpu as pltpu
from jax.sharding import PartitionSpec as P

HEAD = 96
KERNEL = 31
MARGIN = KERNEL // 2
HALO = 16
LANES = 128
EPSILON = 1e-05
LOG2E = 1.4426950408889634

VMEM = pl.BlockSpec(memory_space=pltpu.VMEM)
HBM = pl.BlockSpec(memory_space=pltpu.HBM)
SMEM = pl.BlockSpec(memory_space=pltpu.SMEM)


def params(mebibytes=48):
    return pltpu.CompilerParams(vmem_limit_bytes=mebibytes * 1024 * 1024)


def cost(flops, size, transcendentals=0):
    return pl.CostEstimate(flops=flops, bytes_accessed=size, transcendentals=transcendentals)


def swap_between_chips(x):
    axes = ("seq", "dp")
    pairs = [(i, i + 1) for i in range(1, lax.axis_size(axes) - 1, 2)]
    return lax.ppermute(x, axes, pairs + [(j, i) for i, j in pairs])


def swap_within_chip(x):
    return lax.ppermute(x, "dp", [(0, 1), (1, 0)])


def matmul(left, right):
    return jnp.dot(left, right, preferred_element_type=jnp.float32)


def first_row(rows):
    return (lax.axis_index("seq") * lax.axis_size("dp") + lax.axis_index("dp")) * rows


def ends_of(lengths_ref):
    ends, total = [], jnp.int32(0)
    for i in range(lengths_ref.shape[0]):
        total = total + lengths_ref[i]
        ends.append(total)
    return ends


def ids_of(positions, ends):
    found = jnp.zeros_like(positions)
    for end in ends:
        found = found + (positions >= end).astype(jnp.int32)
    return jnp.where(positions < 0, -1, found)


def project_kernel(
    frames_hbm, gain_hbm, weight_hbm, query_ref, out_ref, frames_buf, gain_buf, weight_buf, normed_ref, sems
):
    rows, model_width = frames_buf.shape
    cols = weight_buf.shape[2]
    half = rows // 2
    copies = []
    for i in range(2):
        span = pl.ds(i * half, half)
        copies.append(pltpu.make_async_copy(frames_hbm.at[span], frames_buf.at[span], sems.at[i]))
    for i in range(3):
        copies.append(pltpu.make_async_copy(weight_hbm.at[(i + 1) % 3], weight_buf.at[i], sems.at[i + 2]))
    gain_copy = pltpu.make_async_copy(gain_hbm, gain_buf, sems.at[5])
    gain_copy.start()
    for copy in copies:
        copy.start()
    gain_copy.wait()
    for i in range(2):
        copies[i].wait()
        span = slice(i * half, (i + 1) * half)
        values = frames_buf[span].astype(jnp.float32)
        centred = values - jnp.mean(values, axis=-1, keepdims=True)
        inverse = lax.rsqrt(jnp.mean(centred * centred, axis=-1, keepdims=True) + EPSILON)
        for j in range(model_width // LANES):
            lanes = slice(j * LANES, (j + 1) * LANES)
            normed_ref[span, lanes] = (centred[:, lanes] * inverse * gain_buf[j : j + 1]).astype(jnp.bfloat16)
    for i in range(2):
        copies[i + 2].wait()
        out_ref[:, i * cols : (i + 1) * cols] = matmul(normed_ref[...], weight_buf[i]).astype(jnp.bfloat16)
    copies[4].wait()
    query_ref[...] = matmul(normed_ref[...], weight_buf[2]).astype(jnp.bfloat16)


def head_window(head):
    low, high = head * HEAD, (head + 1) * HEAD
    left, right = low // LANES * LANES, -(-high // LANES) * LANES
    lane = left + lax.broadcasted_iota(jnp.int32, (1, right - left), 1)
    return left, right, (lane >= low) & (lane < high)


def weights_of(query_ref, side_ref, left, right, mine, same):
    query = jnp.where(mine, query_ref[:, left:right], jnp.zeros((), jnp.bfloat16))
    scores = lax.dot_general(
        query, side_ref[:, left:right], (((1,), (1,)), ((), ())), preferred_element_type=jnp.float32
    )
    return jnp.where(same, jnp.exp2(scores * (HEAD ** (-0.5) * LOG2E)), 0.0)


def same_utterance(lengths_ref, rows, step):
    start = first_row(rows)
    ends = ends_of(lengths_ref)
    query_ids = ids_of(start + lax.broadcasted_iota(jnp.int32, (rows, 1), 0), ends)
    at = start + step * rows
    return query_ids == ids_of(at + lax.broadcasted_iota(jnp.int32, (1, rows), 1), ends)


def place(groups, left, right, mine, rows_value):
    for group in range(left // LANES, right // LANES):
        lanes = slice(group * LANES - left, (group + 1) * LANES - left)
        old, new = groups[group], rows_value[:, lanes]
        groups[group] = new if old is None else jnp.where(mine[:, lanes], new, old)


def weigh_kernel(outward, lengths_ref, query_ref, side_ref, out_ref):
    same = same_utterance(lengths_ref, query_ref.shape[0], outward * (2 * lax.axis_index("dp") - 1))
    for head in range(out_ref.shape[0]):
        left, right, mine = head_window(head)
        out_ref[head] = weights_of(query_ref, side_ref, left, right, mine, same)


def attend_kernel(
    lengths_ref, query_ref, own_weights_ref, outer_ref, own_ref, inner_ref, inner_weights_ref, weight_ref, out_ref
):
    rows, cols = query_ref.shape
    same = same_utterance(lengths_ref, rows, 2 * lax.axis_index("dp") - 1)
    sides = (own_ref, inner_ref, outer_ref)
    groups = [None] * (cols // LANES)
    for head in range(cols // HEAD):
        left, right, mine = head_window(head)
        outer_weights = weights_of(query_ref, outer_ref, left, right, mine, same)
        weights = (own_weights_ref[head], inner_weights_ref[head], outer_weights)
        lane_sums = sum(x[:, i : i + LANES] for x in weights for i in range(0, rows, LANES))
        total = jnp.sum(lane_sums, axis=-1, keepdims=True)
        shift = jnp.where(total > 1.0, 2.0**-20, 2.0**20)
        inverse = 1.0 / (total * shift)
        mixed = None
        for x, side in zip(weights, sides):
            probs = (x * inverse * shift).astype(jnp.bfloat16)
            term = matmul(probs, side[:, cols + left : cols + right])
            mixed = term if mixed is None else mixed + term
        place(groups, left, right, mine, mixed)
    mixed_rows = jnp.concatenate([x.astype(jnp.bfloat16) for x in groups], axis=1)
    chunks, _, width = out_ref.shape
    for chunk in range(chunks):
        part = matmul(mixed_rows, weight_ref[:, chunk * width : (chunk + 1) * width])
        out_ref[chunk] = part.astype(jnp.bfloat16)


def merge_kernel(terms_ref, frames_ref, residual_ref, rounded_ref):
    total = frames_ref[...].astype(jnp.float32)
    for i in range(terms_ref.shape[0]):
        total = total + terms_ref[i].astype(jnp.float32)
    residual_ref[...] = total
    rounded_ref[...] = total.astype(jnp.bfloat16)


def finish_kernel(terms_ref, residual_ref, out_ref):
    total = residual_ref[...]
    for i in range(terms_ref.shape[0]):
        total = total + terms_ref[i].astype(jnp.float32)
    out_ref[...] = total.astype(jnp.bfloat16)


def glu_kernel(residual_ref, gain_ref, weight_ref, out_ref, outer_ref, inner_ref):
    chunks, rows, width = residual_ref.shape
    model_width = chunks * width
    parts = [residual_ref[i].astype(jnp.float32) for i in range(chunks)]
    mean = sum(jnp.sum(x, axis=-1, keepdims=True) for x in parts) / model_width
    parts = [x - mean for x in parts]
    variance = sum(jnp.sum(x * x, axis=-1, keepdims=True) for x in parts) / model_width
    inverse = lax.rsqrt(variance + EPSILON)
    value = gate = None
    for i in range(chunks):
        normed = []
        for j in range(width // LANES):
            at = i * (width // LANES) + j
            lanes = slice(j * LANES, (j + 1) * LANES)
            normed.append((parts[i][:, lanes] * inverse * gain_ref[at : at + 1]).astype(jnp.bfloat16))
        normed = jnp.concatenate(normed, axis=1)
        span = slice(i * width, (i + 1) * width)
        value_term = matmul(normed, weight_ref[0, span])
        gate_term = matmul(normed, weight_ref[1, span])
        value = value_term if value is None else value + value_term
        gate = gate_term if gate is None else gate + gate_term
    gated = (value * jax.nn.sigmoid(gate)).astype(jnp.bfloat16)
    out_ref[...] = gated
    even = lax.axis_index("dp") == 0
    outer_ref[...] = jnp.where(even, gated[:HALO], gated[rows - HALO :])
    inner_ref[...] = jnp.where(even, gated[rows - HALO :], gated[:HALO])


def spans_of(start, count, ends):
    positions = start + lax.broadcasted_iota(jnp.int32, (count, LANES), 0)
    first = jnp.zeros_like(positions)
    last = jnp.zeros_like(positions)
    begin = jnp.int32(0)
    for end in ends:
        inside = (positions >= begin) & (positions < end)
        first = jnp.where(inside, begin - positions, first)
        last = jnp.where(inside, end - 1 - positions, last)
        begin = end
    return first, last


def crossed(start, count, ends):
    found = jnp.bool_(False)
    for end in ends[:-1]:
        found = found | ((end > start - MARGIN) & (end < start + count + MARGIN))
    return found


def convolve(window_ref, base, count, start, ends, taps_ref):
    cols = taps_ref.shape[1]
    first = last = None
    if start is not None:
        first, last = spans_of(start, count, ends)
    running = [jnp.zeros((count, LANES), jnp.float32)] * (cols // LANES)
    for tap in range(KERNEL):
        offset = tap - MARGIN
        at = base + HALO + offset
        keep = None
        if first is not None and offset:
            keep = (first <= offset) if offset < 0 else (last >= offset)
        for group in range(cols // LANES):
            lanes = slice(group * LANES, (group + 1) * LANES)
            term = window_ref[at : at + count, lanes] * taps_ref[tap : tap + 1, lanes]
            if keep is not None:
                term = jnp.where(keep, term, 0.0)
            running[group] = running[group] + term
    return jnp.concatenate([(x * jax.nn.sigmoid(x)).astype(jnp.bfloat16) for x in running], axis=1)


def inside_kernel(lengths_ref, own_ref, taps_ref, out_ref, window_ref):
    start = first_row(own_ref.shape[0]) + HALO
    ends = ends_of(lengths_ref)
    window_ref[...] = own_ref[...].astype(jnp.float32)
    step = 2 * HALO
    mixed = crossed(start, out_ref.shape[0], ends)

    @pl.when(jnp.logical_not(mixed))
    def _():
        for row in range(0, out_ref.shape[0], step):
            out_ref[row : row + step] = convolve(window_ref, row, step, None, ends, taps_ref)

    @pl.when(mixed)
    def _():
        for row in range(0, out_ref.shape[0], step):
            out_ref[row : row + step] = convolve(window_ref, row, step, start + row, ends, taps_ref)


def conv_kernel(
    lengths_ref, outer_ref, inner_ref, own_ref, inside_ref, taps_ref, weight_ref, out_ref, low_ref, high_ref
):
    rows = own_ref.shape[0]
    start = first_row(rows)
    ends = ends_of(lengths_ref)
    even = lax.axis_index("dp") == 0
    low_ref[:HALO] = jnp.where(even, outer_ref[...], inner_ref[...]).astype(jnp.float32)
    low_ref[HALO:] = own_ref[: 2 * HALO].astype(jnp.float32)
    high_ref[: 2 * HALO] = own_ref[rows - 2 * HALO :].astype(jnp.float32)
    high_ref[2 * HALO :] = jnp.where(even, inner_ref[...], outer_ref[...]).astype(jnp.float32)
    low = convolve(low_ref, 0, HALO, start, ends, taps_ref)
    high = convolve(high_ref, 0, HALO, start + rows - HALO, ends, taps_ref)
    activated = jnp.concatenate([low, inside_ref[...], high], axis=0)
    chunks, _, width = out_ref.shape
    for chunk in range(chunks):
        part = matmul(activated, weight_ref[:, chunk * width : (chunk + 1) * width])
        out_ref[chunk] = part.astype(jnp.bfloat16)


def body(
    frames,
    lengths,
    norm_gain,
    qkv_weight,
    out_weight,
    conv_gain,
    glu_weight,
    conv_taps,
    point_weight,
):
    rows, model_width = frames.shape
    group_cols = qkv_weight.shape[2]
    chan_cols = glu_weight.shape[2]
    parts = lax.axis_size("tp")
    out_cols = model_width // parts
    bf16 = jnp.bfloat16
    qkv = jnp.swapaxes(qkv_weight, 0, 1)

    shape = jax.ShapeDtypeStruct

    query, keys_values = pl.pallas_call(
        project_kernel,
        in_specs=[HBM, HBM, HBM],
        out_specs=[VMEM, VMEM],
        out_shape=[shape((rows, group_cols), bf16), shape((rows, 2 * group_cols), bf16)],
        scratch_shapes=[
            pltpu.VMEM((rows, model_width), bf16),
            pltpu.VMEM((model_width // LANES, LANES), jnp.float32),
            pltpu.VMEM((3, model_width, group_cols), bf16),
            pltpu.VMEM((rows, model_width), bf16),
            pltpu.SemaphoreType.DMA((6,)),
        ],
        compiler_params=params(53),
        cost_estimate=cost(6 * rows * model_width * group_cols, 5_000_000),
        name="project",
    )(frames, norm_gain.reshape(-1, LANES), qkv)
    inner = swap_within_chip(keys_values)
    outer = swap_between_chips(keys_values)

    def weigh(outward, side, name):
        return pl.pallas_call(
            functools.partial(weigh_kernel, outward),
            in_specs=[SMEM, VMEM, VMEM],
            out_specs=VMEM,
            out_shape=shape((group_cols // HEAD, rows, rows), jnp.float32),
            compiler_params=params(40),
            cost_estimate=cost(1, 1) if outward else cost(10**9, 2_000_000, 4 * rows * rows),
            name=name,
        )(lengths, query, side)

    own_weights = weigh(0, keys_values, "weigh_own")
    inner_weights = weigh(-1, inner, "weigh_inner")
    attn_terms = pl.pallas_call(
        attend_kernel,
        in_specs=[SMEM] + [VMEM] * 7,
        out_specs=VMEM,
        out_shape=shape((parts, rows, out_cols), bf16),
        compiler_params=params(40),
        cost_estimate=cost(10**9, 4_000_000, 4 * rows * rows),
        name="attend",
    )(lengths, query, own_weights, outer, keys_values, inner, inner_weights, out_weight)
    attn_terms = lax.all_to_all(attn_terms, "tp", 0, 0, tiled=True)
    own_frames = lax.dynamic_slice_in_dim(frames, lax.axis_index("tp") * out_cols, out_cols, 1)
    residual, rounded = pl.pallas_call(
        merge_kernel,
        in_specs=[VMEM] * 2,
        out_specs=[VMEM] * 2,
        out_shape=[shape((rows, out_cols), jnp.float32), shape((rows, out_cols), bf16)],
        compiler_params=params(40),
        cost_estimate=cost(10**6, 2_000_000),
        name="merge",
    )(attn_terms, own_frames)
    gathered = lax.all_gather(rounded, "tp", axis=0)
    gated, outer_rows, inner_rows = pl.pallas_call(
        glu_kernel,
        in_specs=[VMEM] * 3,
        out_specs=[VMEM] * 3,
        out_shape=[shape((rows, chan_cols), bf16)] + [shape((HALO, chan_cols), bf16)] * 2,
        compiler_params=params(),
        cost_estimate=cost(4 * rows * model_width * chan_cols, 3_500_000),
        name="glu",
    )(gathered, conv_gain.reshape(-1, LANES), jnp.swapaxes(glu_weight, 0, 1))
    outer_rows = swap_between_chips(outer_rows)
    inner_rows = swap_within_chip(inner_rows)
    inside = pl.pallas_call(
        inside_kernel,
        in_specs=[SMEM, VMEM, VMEM],
        out_specs=VMEM,
        out_shape=shape((rows - 2 * HALO, chan_cols), bf16),
        scratch_shapes=[pltpu.VMEM((rows, chan_cols), jnp.float32)],
        compiler_params=params(),
        cost_estimate=cost(10**9, 4_000_000),
        name="inside",
    )(lengths, gated, conv_taps)
    conv_terms = pl.pallas_call(
        conv_kernel,
        in_specs=[SMEM] + [VMEM] * 6,
        out_specs=VMEM,
        out_shape=shape((parts, rows, out_cols), bf16),
        scratch_shapes=[pltpu.VMEM((3 * HALO, chan_cols), jnp.float32)] * 2,
        compiler_params=params(),
        cost_estimate=cost(2 * rows * model_width * chan_cols, 2_500_000),
        name="conv",
    )(lengths, outer_rows, inner_rows, gated, inside, conv_taps, point_weight)
    conv_terms = lax.all_to_all(conv_terms, "tp", 0, 0, tiled=True)
    return pl.pallas_call(
        finish_kernel,
        in_specs=[VMEM] * 2,
        out_specs=VMEM,
        out_shape=shape((rows, out_cols), bf16),
        compiler_params=params(40),
        cost_estimate=cost(10**6, 2_000_000),
        name="finish",
    )(conv_terms, residual)


def solution(mesh):
    return jax.shard_map(
        body,
        mesh=mesh,
        in_specs=(
            P(("seq", "dp"), None),
            P(),
            P(),
            P(None, None, "tp"),
            P("tp", None),
            P(),
            P(None, None, "tp"),
            P(None, "tp"),
            P("tp", None),
        ),
        out_specs=P(("seq", "dp"), "tp"),
        check_vma=False,
    )
```

```python
import functools

import jax
import jax.numpy as jnp
from jax import lax
from jax.experimental import pallas as pl
from jax.experimental.pallas import tpu as pltpu
from jax.sharding import PartitionSpec as P

HEAD = 96
KERNEL = 31
MARGIN = KERNEL // 2
HALO = 16
LANES = 128
EPSILON = 1e-05
LOG2E = 1.4426950408889634

VMEM = pl.BlockSpec(memory_space=pltpu.VMEM)
HBM = pl.BlockSpec(memory_space=pltpu.HBM)
SMEM = pl.BlockSpec(memory_space=pltpu.SMEM)


def params(mebibytes=20):
    return pltpu.CompilerParams(vmem_limit_bytes=mebibytes * 1024 * 1024)


def cost(flops, size, transcendentals=0):
    return pl.CostEstimate(flops=flops, bytes_accessed=size, transcendentals=transcendentals)


def swap_between_chips(x):
    axes = ("seq", "dp")
    pairs = [(i, i + 1) for i in range(1, lax.axis_size(axes) - 1, 2)]
    return lax.ppermute(x, axes, pairs + [(j, i) for i, j in pairs])


def swap_within_chip(x):
    return lax.ppermute(x, "dp", [(0, 1), (1, 0)])


def matmul(left, right):
    return jnp.dot(left, right, preferred_element_type=jnp.float32)


def first_row(rows):
    return (lax.axis_index("seq") * lax.axis_size("dp") + lax.axis_index("dp")) * rows


def ends_of(lengths_ref):
    ends, total = [], jnp.int32(0)
    for i in range(lengths_ref.shape[0]):
        total = total + lengths_ref[i]
        ends.append(total)
    return ends


def ids_of(positions, ends):
    found = jnp.zeros_like(positions)
    for end in ends:
        found = found + (positions >= end).astype(jnp.int32)
    return jnp.where(positions < 0, -1, found)


def project_kernel(
    frames_hbm, gain_hbm, weight_hbm, query_ref, out_ref, edge_ref, frames_buf, gain_buf, weight_buf, normed_ref, sems
):
    rows, model_width = frames_buf.shape
    cols = weight_buf.shape[2]
    half = rows // 2
    copies = []
    for i in range(2):
        span = pl.ds(i * half, half)
        copies.append(pltpu.make_async_copy(frames_hbm.at[span], frames_buf.at[span], sems.at[i]))
    for i in range(3):
        copies.append(pltpu.make_async_copy(weight_hbm.at[(i + 1) % 3], weight_buf.at[i], sems.at[i + 2]))
    gain_copy = pltpu.make_async_copy(gain_hbm, gain_buf, sems.at[5])
    gain_copy.start()
    for copy in copies:
        copy.start()
    gain_copy.wait()
    for i in range(2):
        copies[i].wait()
        span = slice(i * half, (i + 1) * half)
        values = frames_buf[span].astype(jnp.float32)
        centred = values - jnp.mean(values, axis=-1, keepdims=True)
        inverse = lax.rsqrt(jnp.mean(centred * centred, axis=-1, keepdims=True) + EPSILON)
        for j in range(model_width // LANES):
            lanes = slice(j * LANES, (j + 1) * LANES)
            normed_ref[span, lanes] = (centred[:, lanes] * inverse * gain_buf[j : j + 1]).astype(jnp.bfloat16)
    edge_ref[:HALO] = frames_buf[:HALO]
    edge_ref[HALO:] = frames_buf[rows - HALO :]
    for i in range(2):
        copies[i + 2].wait()
        out_ref[:, i * cols : (i + 1) * cols] = matmul(normed_ref[...], weight_buf[i]).astype(jnp.bfloat16)
    copies[4].wait()
    query_ref[...] = matmul(normed_ref[...], weight_buf[2]).astype(jnp.bfloat16)


def head_window(head):
    low, high = head * HEAD, (head + 1) * HEAD
    left, right = low // LANES * LANES, -(-high // LANES) * LANES
    lane = left + lax.broadcasted_iota(jnp.int32, (1, right - left), 1)
    return left, right, (lane >= low) & (lane < high)


def weights_of(query_ref, side_ref, left, right, mine, same):
    query = jnp.where(mine, query_ref[:, left:right], jnp.zeros((), jnp.bfloat16))
    scores = lax.dot_general(
        query, side_ref[:, left:right], (((1,), (1,)), ((), ())), preferred_element_type=jnp.float32
    )
    return jnp.where(same, jnp.exp2(scores * (HEAD ** (-0.5) * LOG2E)), 0.0)


def same_utterance(lengths_ref, rows, step):
    start = first_row(rows)
    ends = ends_of(lengths_ref)
    query_ids = ids_of(start + lax.broadcasted_iota(jnp.int32, (rows, 1), 0), ends)
    at = start + step * rows
    return query_ids == ids_of(at + lax.broadcasted_iota(jnp.int32, (1, rows), 1), ends)


def place(groups, left, right, mine, rows_value):
    for group in range(left // LANES, right // LANES):
        lanes = slice(group * LANES - left, (group + 1) * LANES - left)
        old, new = groups[group], rows_value[:, lanes]
        groups[group] = new if old is None else jnp.where(mine[:, lanes], new, old)


def weigh_kernel(outward, lengths_ref, query_ref, side_ref, out_ref):
    same = same_utterance(lengths_ref, query_ref.shape[0], outward * (2 * lax.axis_index("dp") - 1))
    for head in range(out_ref.shape[0]):
        left, right, mine = head_window(head)
        out_ref[head] = weights_of(query_ref, side_ref, left, right, mine, same)


def attend_kernel(
    lengths_ref, query_ref, own_weights_ref, outer_ref, own_ref, inner_ref, inner_weights_ref, weight_ref, edge_ref,
    out_ref, outward_ref,
):
    rows, cols = query_ref.shape
    same = same_utterance(lengths_ref, rows, 2 * lax.axis_index("dp") - 1)
    sides = (own_ref, inner_ref, outer_ref)
    groups = [None] * (cols // LANES)
    for head in range(cols // HEAD):
        left, right, mine = head_window(head)
        outer_weights = weights_of(query_ref, outer_ref, left, right, mine, same)
        weights = (own_weights_ref[head], inner_weights_ref[head], outer_weights)
        lane_sums = sum(x[:, i : i + LANES] for x in weights for i in range(0, rows, LANES))
        total = jnp.sum(lane_sums, axis=-1, keepdims=True)
        shift = jnp.where(total > 1.0, 2.0**-20, 2.0**20)
        inverse = 1.0 / (total * shift)
        mixed = None
        for x, side in zip(weights, sides):
            probs = (x * inverse * shift).astype(jnp.bfloat16)
            term = matmul(probs, side[:, cols + left : cols + right])
            mixed = term if mixed is None else mixed + term
        place(groups, left, right, mine, mixed)
    mixed_rows = jnp.concatenate([x.astype(jnp.bfloat16) for x in groups], axis=1)
    even = lax.axis_index("dp") == 0
    outward_ref[:, :cols] = jnp.where(even, mixed_rows[:HALO], mixed_rows[rows - HALO :])
    outward_ref[:, cols:] = jnp.where(even, edge_ref[:HALO], edge_ref[HALO:])
    chunks, _, width = out_ref.shape
    for chunk in range(chunks):
        part = matmul(mixed_rows, weight_ref[:, chunk * width : (chunk + 1) * width])
        out_ref[chunk] = part.astype(jnp.bfloat16)


def edge_kernel(outer_ref, weight_ref, out_ref):
    mixed = outer_ref[:, : weight_ref.shape[0]]
    chunks, _, width = out_ref.shape
    for chunk in range(chunks):
        part = matmul(mixed, weight_ref[:, chunk * width : (chunk + 1) * width])
        out_ref[chunk] = part.astype(jnp.bfloat16)


def merge_kernel(terms_ref, frames_ref, edge_terms_ref, residual_ref, out_ref):
    rows = frames_ref.shape[0]
    total = frames_ref[...].astype(jnp.float32)
    chunks, edge_rows, _ = edge_terms_ref.shape
    for i in range(chunks):
        total = total + terms_ref[i].astype(jnp.float32)
        out_ref[rows + i * edge_rows : rows + (i + 1) * edge_rows] = edge_terms_ref[i]
    residual_ref[...] = total
    out_ref[:rows] = total.astype(jnp.bfloat16)


def finish_kernel(terms_ref, residual_ref, out_ref):
    total = residual_ref[...]
    for i in range(terms_ref.shape[0]):
        total = total + terms_ref[i].astype(jnp.float32)
    out_ref[...] = total.astype(jnp.bfloat16)


def normalise(parts, gain_ref):
    model_width = sum(x.shape[1] for x in parts)
    mean = sum(jnp.sum(x, axis=-1, keepdims=True) for x in parts) / model_width
    parts = [x - mean for x in parts]
    variance = sum(jnp.sum(x * x, axis=-1, keepdims=True) for x in parts) / model_width
    inverse = lax.rsqrt(variance + EPSILON)
    normed, at = [], 0
    for x in parts:
        lanes = []
        for j in range(0, x.shape[1], LANES):
            lanes.append((x[:, j : j + LANES] * inverse * gain_ref[at : at + 1]).astype(jnp.bfloat16))
            at += 1
        normed.append(jnp.concatenate(lanes, axis=1))
    return normed


def glu_kernel(gathered_ref, edge_ref, gain_ref, weight_ref, out_ref, outer_ref, inner_ref):
    chunks, _, width = gathered_ref.shape
    rows = out_ref.shape[0]
    first = edge_ref.shape[1] - chunks * width
    outer = []
    for i in range(chunks):
        at = rows + i * HALO
        total = edge_ref[:, first + i * width : first + (i + 1) * width].astype(jnp.float32)
        for j in range(chunks):
            total = total + gathered_ref[j, at : at + HALO].astype(jnp.float32)
        outer.append(total)
    outer = normalise(outer, gain_ref)
    own = normalise([gathered_ref[i, :rows].astype(jnp.float32) for i in range(chunks)], gain_ref)
    value = gate = None
    for i in range(chunks):
        normed = jnp.concatenate([own[i], outer[i]], axis=0)
        span = slice(i * width, (i + 1) * width)
        value_term = matmul(normed, weight_ref[0, span])
        gate_term = matmul(normed, weight_ref[1, span])
        value = value_term if value is None else value + value_term
        gate = gate_term if gate is None else gate + gate_term
    gated = (value * jax.nn.sigmoid(gate)).astype(jnp.bfloat16)
    out_ref[...] = gated[:rows]
    outer_ref[...] = gated[rows:]
    even = lax.axis_index("dp") == 0
    inner_ref[...] = jnp.where(even, gated[rows - HALO : rows], gated[:HALO])


def spans_of(start, count, ends):
    positions = start + lax.broadcasted_iota(jnp.int32, (count, LANES), 0)
    first = jnp.zeros_like(positions)
    last = jnp.zeros_like(positions)
    begin = jnp.int32(0)
    for end in ends:
        inside = (positions >= begin) & (positions < end)
        first = jnp.where(inside, begin - positions, first)
        last = jnp.where(inside, end - 1 - positions, last)
        begin = end
    return first, last


def crossed(start, count, ends):
    found = jnp.bool_(False)
    for end in ends[:-1]:
        found = found | ((end > start - MARGIN) & (end < start + count + MARGIN))
    return found


def convolve_one(window_ref, taps_ref, sums_ref, out_ref):
    rows, cols = out_ref.shape
    count = sums_ref.shape[1]
    step = 2 * HALO
    for lane in range(0, cols, LANES):
        lanes = slice(lane, lane + LANES)
        for shift in range(8):
            total = None
            for at in range(0, KERNEL + 1 - shift, 8):
                tap = at + shift - 1
                if tap < 0:
                    continue
                term = window_ref[at : at + count, lanes] * taps_ref[tap : tap + 1, lanes]
                total = term if total is None else total + term
            sums_ref[shift, :, lanes] = total
        for row in range(0, rows, step):
            total = sums_ref[0, row : row + step, lanes]
            for shift in range(1, 8):
                total = total + sums_ref[shift, row + shift : row + shift + step, lanes]
            out_ref[row : row + step, lanes] = (total * jax.nn.sigmoid(total)).astype(jnp.bfloat16)


def convolve(window_ref, base, count, start, ends, taps_ref):
    cols = taps_ref.shape[1]
    first, last = spans_of(start, count, ends)
    running = [jnp.zeros((count, LANES), jnp.float32)] * (cols // LANES)
    for tap in range(KERNEL):
        offset = tap - MARGIN
        at = base + HALO + offset
        keep = None if offset == 0 else (first <= offset) if offset < 0 else (last >= offset)
        for group in range(cols // LANES):
            lanes = slice(group * LANES, (group + 1) * LANES)
            term = window_ref[at : at + count, lanes] * taps_ref[tap : tap + 1, lanes]
            if keep is not None:
                term = jnp.where(keep, term, 0.0)
            running[group] = running[group] + term
    return jnp.concatenate([(x * jax.nn.sigmoid(x)).astype(jnp.bfloat16) for x in running], axis=1)


def inside_kernel(lengths_ref, own_ref, taps_ref, out_ref, window_ref, sums_ref):
    start = first_row(own_ref.shape[0]) + HALO
    ends = ends_of(lengths_ref)
    window_ref[...] = own_ref[...].astype(jnp.float32)
    step = 2 * HALO
    mixed = crossed(start, out_ref.shape[0], ends)

    @pl.when(jnp.logical_not(mixed))
    def _():
        convolve_one(window_ref, taps_ref, sums_ref, out_ref)

    @pl.when(mixed)
    def _():
        for row in range(0, out_ref.shape[0], step):
            out_ref[row : row + step] = convolve(window_ref, row, step, start + row, ends, taps_ref)


def conv_kernel(
    lengths_ref, outer_ref, inner_ref, own_ref, inside_ref, taps_ref, weight_ref, out_ref, low_ref, high_ref
):
    rows = own_ref.shape[0]
    start = first_row(rows)
    ends = ends_of(lengths_ref)
    even = lax.axis_index("dp") == 0
    low_ref[:HALO] = jnp.where(even, outer_ref[...], inner_ref[...]).astype(jnp.float32)
    low_ref[HALO:] = own_ref[: 2 * HALO].astype(jnp.float32)
    high_ref[: 2 * HALO] = own_ref[rows - 2 * HALO :].astype(jnp.float32)
    high_ref[2 * HALO :] = jnp.where(even, inner_ref[...], outer_ref[...]).astype(jnp.float32)
    low = convolve(low_ref, 0, HALO, start, ends, taps_ref)
    high = convolve(high_ref, 0, HALO, start + rows - HALO, ends, taps_ref)
    activated = jnp.concatenate([low, inside_ref[...], high], axis=0)
    chunks, _, width = out_ref.shape
    for chunk in range(chunks):
        part = matmul(activated, weight_ref[:, chunk * width : (chunk + 1) * width])
        out_ref[chunk] = part.astype(jnp.bfloat16)


def body(
    frames,
    lengths,
    norm_gain,
    qkv_weight,
    out_weight,
    conv_gain,
    glu_weight,
    conv_taps,
    point_weight,
):
    rows, model_width = frames.shape
    group_cols = qkv_weight.shape[2]
    chan_cols = glu_weight.shape[2]
    parts = lax.axis_size("tp")
    out_cols = model_width // parts
    bf16 = jnp.bfloat16
    qkv = jnp.swapaxes(qkv_weight, 0, 1)

    shape = jax.ShapeDtypeStruct

    query, keys_values, edges = pl.pallas_call(
        project_kernel,
        in_specs=[HBM, HBM, HBM],
        out_specs=[VMEM] * 3,
        out_shape=[
            shape((rows, group_cols), bf16),
            shape((rows, 2 * group_cols), bf16),
            shape((2 * HALO, model_width), bf16),
        ],
        scratch_shapes=[
            pltpu.VMEM((rows, model_width), bf16),
            pltpu.VMEM((model_width // LANES, LANES), jnp.float32),
            pltpu.VMEM((3, model_width, group_cols), bf16),
            pltpu.VMEM((rows, model_width), bf16),
            pltpu.SemaphoreType.DMA((6,)),
        ],
        compiler_params=params(53),
        cost_estimate=cost(6 * rows * model_width * group_cols, 5_000_000),
        name="project",
    )(frames, norm_gain.reshape(-1, LANES), qkv)
    inner = swap_within_chip(keys_values)
    outer = swap_between_chips(keys_values)

    def weigh(outward, side, name):
        return pl.pallas_call(
            functools.partial(weigh_kernel, outward),
            in_specs=[SMEM, VMEM, VMEM],
            out_specs=VMEM,
            out_shape=shape((group_cols // HEAD, rows, rows), jnp.float32),
            compiler_params=params(16),
            cost_estimate=cost(1, 1) if outward else cost(10**9, 2_000_000, 4 * rows * rows),
            name=name,
        )(lengths, query, side)

    own_weights = weigh(0, keys_values, "weigh_own")
    inner_weights = weigh(-1, inner, "weigh_inner")
    message = shape((HALO, group_cols + model_width), bf16)
    attn_terms, outward = pl.pallas_call(
        attend_kernel,
        in_specs=[SMEM] + [VMEM] * 8,
        out_specs=[VMEM] * 2,
        out_shape=[shape((parts, rows, out_cols), bf16), message],
        compiler_params=params(16),
        cost_estimate=cost(10**9, 4_000_000, 4 * rows * rows),
        name="attend",
    )(lengths, query, own_weights, outer, keys_values, inner, inner_weights, out_weight, edges)
    attn_terms = lax.all_to_all(attn_terms, "tp", 0, 0, tiled=True)
    outer_edge = swap_between_chips(outward)
    own_frames = lax.dynamic_slice_in_dim(frames, lax.axis_index("tp") * out_cols, out_cols, 1)
    edge_terms = pl.pallas_call(
        edge_kernel,
        in_specs=[VMEM] * 2,
        out_specs=VMEM,
        out_shape=shape((parts, HALO, out_cols), bf16),
        compiler_params=params(16),
        cost_estimate=cost(10**8, 2_000_000),
        name="edge",
    )(outer_edge, out_weight)
    residual, rounded = pl.pallas_call(
        merge_kernel,
        in_specs=[VMEM] * 3,
        out_specs=[VMEM] * 2,
        out_shape=[shape((rows, out_cols), jnp.float32), shape((rows + parts * HALO, out_cols), bf16)],
        compiler_params=params(16),
        cost_estimate=cost(10**6, 2_000_000),
        name="merge",
    )(attn_terms, own_frames, edge_terms)
    gathered = lax.all_gather(rounded, "tp", axis=0)
    gated, outer_rows, inner_rows = pl.pallas_call(
        glu_kernel,
        in_specs=[VMEM] * 4,
        out_specs=[VMEM] * 3,
        out_shape=[shape((rows, chan_cols), bf16)] + [shape((HALO, chan_cols), bf16)] * 2,
        compiler_params=params(),
        cost_estimate=cost(4 * rows * model_width * chan_cols, 3_500_000),
        name="glu",
    )(gathered, outer_edge, conv_gain.reshape(-1, LANES), jnp.swapaxes(glu_weight, 0, 1))
    inner_rows = swap_within_chip(inner_rows)
    inside = pl.pallas_call(
        inside_kernel,
        in_specs=[SMEM, VMEM, VMEM],
        out_specs=VMEM,
        out_shape=shape((rows - 2 * HALO, chan_cols), bf16),
        scratch_shapes=[
            pltpu.VMEM((rows, chan_cols), jnp.float32),
            pltpu.VMEM((8, rows - 3 * HALO // 2, chan_cols), jnp.float32),
        ],
        compiler_params=params(),
        cost_estimate=cost(10**9, 4_000_000),
        name="inside",
    )(lengths, gated, conv_taps)
    conv_terms = pl.pallas_call(
        conv_kernel,
        in_specs=[SMEM] + [VMEM] * 6,
        out_specs=VMEM,
        out_shape=shape((parts, rows, out_cols), bf16),
        scratch_shapes=[pltpu.VMEM((3 * HALO, chan_cols), jnp.float32)] * 2,
        compiler_params=params(),
        cost_estimate=cost(2 * rows * model_width * chan_cols, 2_500_000),
        name="conv",
    )(lengths, outer_rows, inner_rows, gated, inside, conv_taps, point_weight)
    conv_terms = lax.all_to_all(conv_terms, "tp", 0, 0, tiled=True)
    return pl.pallas_call(
        finish_kernel,
        in_specs=[VMEM] * 2,
        out_specs=VMEM,
        out_shape=shape((rows, out_cols), bf16),
        compiler_params=params(16),
        cost_estimate=cost(10**6, 2_000_000),
        name="finish",
    )(conv_terms, residual)


def solution(mesh):
    return jax.shard_map(
        body,
        mesh=mesh,
        in_specs=(
            P(("seq", "dp"), None),
            P(),
            P(),
            P(None, None, "tp"),
            P("tp", None),
            P(),
            P(None, None, "tp"),
            P(None, "tp"),
            P("tp", None),
        ),
        out_specs=P(("seq", "dp"), "tp"),
        check_vma=False,
    )
```

```python
import jax
import jax.numpy as jnp
from jax import lax
from jax.experimental import pallas as pl
from jax.experimental.pallas import tpu as pltpu
from jax.sharding import PartitionSpec as P

HEAD = 96
KERNEL = 31
MARGIN = KERNEL // 2
HALO = 16
LANES = 128
EPSILON = 1e-05
LOG2E = 1.4426950408889634

VMEM = pl.BlockSpec(memory_space=pltpu.VMEM)
HBM = pl.BlockSpec(memory_space=pltpu.HBM)
SMEM = pl.BlockSpec(memory_space=pltpu.SMEM)


def params(mebibytes=20):
    return pltpu.CompilerParams(vmem_limit_bytes=mebibytes * 1024 * 1024)


def cost(flops, size, transcendentals=0):
    return pl.CostEstimate(flops=flops, bytes_accessed=size, transcendentals=transcendentals)


def swap_between_chips(x):
    axes = ("seq", "dp")
    pairs = [(i, i + 1) for i in range(1, lax.axis_size(axes) - 1, 2)]
    return lax.ppermute(x, axes, pairs + [(j, i) for i, j in pairs])


def swap_within_chip(x):
    return lax.ppermute(x, "dp", [(0, 1), (1, 0)])


def matmul(left, right):
    return jnp.dot(left, right, preferred_element_type=jnp.float32)


def first_row(rows):
    return (lax.axis_index("seq") * lax.axis_size("dp") + lax.axis_index("dp")) * rows


def ends_of(lengths_ref):
    ends, total = [], jnp.int32(0)
    for i in range(lengths_ref.shape[0]):
        total = total + lengths_ref[i]
        ends.append(total)
    return ends


def ids_of(positions, ends):
    found = jnp.zeros_like(positions)
    for end in ends:
        found = found + (positions >= end).astype(jnp.int32)
    return jnp.where(positions < 0, -1, found)


def project_kernel(
    frames_hbm, gain_hbm, weight_hbm, query_ref, out_ref, frames_buf, gain_buf, weight_buf, normed_ref, sems
):
    rows, model_width = frames_buf.shape
    cols = weight_buf.shape[2]
    half = rows // 2
    copies = []
    for i in range(2):
        span = pl.ds(i * half, half)
        copies.append(pltpu.make_async_copy(frames_hbm.at[span], frames_buf.at[span], sems.at[i]))
    for i in range(3):
        copies.append(pltpu.make_async_copy(weight_hbm.at[(i + 1) % 3], weight_buf.at[i], sems.at[i + 2]))
    gain_copy = pltpu.make_async_copy(gain_hbm, gain_buf, sems.at[5])
    gain_copy.start()
    for copy in copies:
        copy.start()
    gain_copy.wait()
    for i in range(2):
        copies[i].wait()
        span = slice(i * half, (i + 1) * half)
        values = frames_buf[span].astype(jnp.float32)
        centred = values - jnp.mean(values, axis=-1, keepdims=True)
        inverse = lax.rsqrt(jnp.mean(centred * centred, axis=-1, keepdims=True) + EPSILON)
        for j in range(model_width // LANES):
            lanes = slice(j * LANES, (j + 1) * LANES)
            normed_ref[span, lanes] = (centred[:, lanes] * inverse * gain_buf[j : j + 1]).astype(jnp.bfloat16)
    for i in range(2):
        copies[i + 2].wait()
        out_ref[:, i * cols : (i + 1) * cols] = matmul(normed_ref[...], weight_buf[i]).astype(jnp.bfloat16)
    copies[4].wait()
    query_ref[...] = matmul(normed_ref[...], weight_buf[2]).astype(jnp.bfloat16)


def head_window(head):
    low, high = head * HEAD, (head + 1) * HEAD
    left, right = low // LANES * LANES, -(-high // LANES) * LANES
    lane = left + lax.broadcasted_iota(jnp.int32, (1, right - left), 1)
    return left, right, (lane >= low) & (lane < high)


def weights_of(query_ref, side_ref, left, right, mine, same):
    query = jnp.where(mine, query_ref[:, left:right], jnp.zeros((), jnp.bfloat16))
    scores = lax.dot_general(
        query, side_ref[:, left:right], (((1,), (1,)), ((), ())), preferred_element_type=jnp.float32
    )
    return jnp.where(same, jnp.exp2(scores * (HEAD ** (-0.5) * LOG2E)), 0.0)


def same_utterance(lengths_ref, rows, step):
    start = first_row(rows)
    ends = ends_of(lengths_ref)
    query_ids = ids_of(start + lax.broadcasted_iota(jnp.int32, (rows, 1), 0), ends)
    at = start + step * rows
    return query_ids == ids_of(at + lax.broadcasted_iota(jnp.int32, (1, rows), 1), ends)


def place(groups, left, right, mine, rows_value):
    for group in range(left // LANES, right // LANES):
        lanes = slice(group * LANES - left, (group + 1) * LANES - left)
        old, new = groups[group], rows_value[:, lanes]
        groups[group] = new if old is None else jnp.where(mine[:, lanes], new, old)


def weigh_kernel(lengths_ref, query_ref, side_ref, out_ref):
    same = same_utterance(lengths_ref, query_ref.shape[0], 0)
    for head in range(out_ref.shape[0]):
        left, right, mine = head_window(head)
        out_ref[head] = weights_of(query_ref, side_ref, left, right, mine, same)


def attend_kernel(
    lengths_ref, query_ref, own_weights_ref, own_ref, inner_ref, outer_ref, weight_ref, out_ref
):
    rows, cols = query_ref.shape
    outward = 2 * lax.axis_index("dp") - 1
    same_outer = same_utterance(lengths_ref, rows, outward)
    same_inner = same_utterance(lengths_ref, rows, -outward)
    sides = (own_ref, inner_ref, outer_ref)
    groups = [None] * (cols // LANES)
    for head in range(cols // HEAD):
        left, right, mine = head_window(head)
        inner_weights = weights_of(query_ref, inner_ref, left, right, mine, same_inner)
        outer_weights = weights_of(query_ref, outer_ref, left, right, mine, same_outer)
        weights = (own_weights_ref[head], inner_weights, outer_weights)
        lane_sums = sum(x[:, i : i + LANES] for x in weights for i in range(0, rows, LANES))
        total = jnp.sum(lane_sums, axis=-1, keepdims=True)
        shift = jnp.where(total > 1.0, 2.0**-20, 2.0**20)
        inverse = 1.0 / (total * shift)
        mixed = None
        for x, side in zip(weights, sides):
            probs = (x * inverse * shift).astype(jnp.bfloat16)
            term = matmul(probs, side[:, cols + left : cols + right])
            mixed = term if mixed is None else mixed + term
        place(groups, left, right, mine, mixed)
    mixed_rows = jnp.concatenate([x.astype(jnp.bfloat16) for x in groups], axis=1)
    chunks, _, width = out_ref.shape
    for chunk in range(chunks):
        part = matmul(mixed_rows, weight_ref[:, chunk * width : (chunk + 1) * width])
        out_ref[chunk] = part.astype(jnp.bfloat16)


def merge_kernel(terms_ref, frames_ref, residual_ref, rounded_ref):
    total = frames_ref[...].astype(jnp.float32)
    for i in range(terms_ref.shape[0]):
        total = total + terms_ref[i].astype(jnp.float32)
    residual_ref[...] = total
    rounded_ref[...] = total.astype(jnp.bfloat16)


def finish_kernel(terms_ref, residual_ref, out_ref):
    total = residual_ref[...]
    for i in range(terms_ref.shape[0]):
        total = total + terms_ref[i].astype(jnp.float32)
    out_ref[...] = total.astype(jnp.bfloat16)


def glu_kernel(residual_ref, gain_ref, weight_ref, out_ref, outer_ref, inner_ref):
    chunks, rows, width = residual_ref.shape
    model_width = chunks * width
    parts = [residual_ref[i].astype(jnp.float32) for i in range(chunks)]
    mean = sum(jnp.sum(x, axis=-1, keepdims=True) for x in parts) / model_width
    parts = [x - mean for x in parts]
    variance = sum(jnp.sum(x * x, axis=-1, keepdims=True) for x in parts) / model_width
    inverse = lax.rsqrt(variance + EPSILON)
    value = gate = None
    for i in range(chunks):
        normed = []
        for j in range(width // LANES):
            at = i * (width // LANES) + j
            lanes = slice(j * LANES, (j + 1) * LANES)
            normed.append((parts[i][:, lanes] * inverse * gain_ref[at : at + 1]).astype(jnp.bfloat16))
        normed = jnp.concatenate(normed, axis=1)
        span = slice(i * width, (i + 1) * width)
        value_term = matmul(normed, weight_ref[0, span])
        gate_term = matmul(normed, weight_ref[1, span])
        value = value_term if value is None else value + value_term
        gate = gate_term if gate is None else gate + gate_term
    gated = (value * jax.nn.sigmoid(gate)).astype(jnp.bfloat16)
    out_ref[...] = gated
    even = lax.axis_index("dp") == 0
    outer_ref[...] = jnp.where(even, gated[:HALO], gated[rows - HALO :])
    inner_ref[...] = jnp.where(even, gated[rows - HALO :], gated[:HALO])


def spans_of(start, count, ends):
    positions = start + lax.broadcasted_iota(jnp.int32, (count, LANES), 0)
    first = jnp.zeros_like(positions)
    last = jnp.zeros_like(positions)
    begin = jnp.int32(0)
    for end in ends:
        inside = (positions >= begin) & (positions < end)
        first = jnp.where(inside, begin - positions, first)
        last = jnp.where(inside, end - 1 - positions, last)
        begin = end
    return first, last


def crossed(start, count, ends):
    found = jnp.bool_(False)
    for end in ends[:-1]:
        found = found | ((end > start - MARGIN) & (end < start + count + MARGIN))
    return found


def convolve_one(window_ref, taps_ref, sums_ref, out_ref):
    rows, cols = out_ref.shape
    count = sums_ref.shape[1]
    step = 2 * HALO
    for lane in range(0, cols, LANES):
        lanes = slice(lane, lane + LANES)
        for shift in range(8):
            total = None
            for at in range(0, KERNEL + 1 - shift, 8):
                tap = at + shift - 1
                if tap < 0:
                    continue
                term = window_ref[at : at + count, lanes] * taps_ref[tap : tap + 1, lanes]
                total = term if total is None else total + term
            sums_ref[shift, :, lanes] = total
        for row in range(0, rows, step):
            total = sums_ref[0, row : row + step, lanes]
            for shift in range(1, 8):
                total = total + sums_ref[shift, row + shift : row + shift + step, lanes]
            out_ref[row : row + step, lanes] = (total * jax.nn.sigmoid(total)).astype(jnp.bfloat16)


def convolve(window_ref, base, count, start, ends, taps_ref):
    cols = taps_ref.shape[1]
    first, last = spans_of(start, count, ends)
    running = [jnp.zeros((count, LANES), jnp.float32)] * (cols // LANES)
    for tap in range(KERNEL):
        offset = tap - MARGIN
        at = base + HALO + offset
        keep = None if offset == 0 else (first <= offset) if offset < 0 else (last >= offset)
        for group in range(cols // LANES):
            lanes = slice(group * LANES, (group + 1) * LANES)
            term = window_ref[at : at + count, lanes] * taps_ref[tap : tap + 1, lanes]
            if keep is not None:
                term = jnp.where(keep, term, 0.0)
            running[group] = running[group] + term
    return jnp.concatenate([(x * jax.nn.sigmoid(x)).astype(jnp.bfloat16) for x in running], axis=1)


def inside_kernel(lengths_ref, own_ref, taps_ref, out_ref, window_ref, sums_ref):
    start = first_row(own_ref.shape[0]) + HALO
    ends = ends_of(lengths_ref)
    window_ref[...] = own_ref[...].astype(jnp.float32)
    step = 2 * HALO
    mixed = crossed(start, out_ref.shape[0], ends)

    @pl.when(jnp.logical_not(mixed))
    def _():
        convolve_one(window_ref, taps_ref, sums_ref, out_ref)

    @pl.when(mixed)
    def _():
        for row in range(0, out_ref.shape[0], step):
            out_ref[row : row + step] = convolve(window_ref, row, step, start + row, ends, taps_ref)


def conv_kernel(
    lengths_ref, outer_ref, inner_ref, own_ref, inside_ref, taps_ref, weight_ref, out_ref, low_ref, high_ref
):
    rows = own_ref.shape[0]
    start = first_row(rows)
    ends = ends_of(lengths_ref)
    even = lax.axis_index("dp") == 0
    low_ref[:HALO] = jnp.where(even, outer_ref[...], inner_ref[...]).astype(jnp.float32)
    low_ref[HALO:] = own_ref[: 2 * HALO].astype(jnp.float32)
    high_ref[: 2 * HALO] = own_ref[rows - 2 * HALO :].astype(jnp.float32)
    high_ref[2 * HALO :] = jnp.where(even, inner_ref[...], outer_ref[...]).astype(jnp.float32)
    low = convolve(low_ref, 0, HALO, start, ends, taps_ref)
    high = convolve(high_ref, 0, HALO, start + rows - HALO, ends, taps_ref)
    activated = jnp.concatenate([low, inside_ref[...], high], axis=0)
    chunks, _, width = out_ref.shape
    for chunk in range(chunks):
        part = matmul(activated, weight_ref[:, chunk * width : (chunk + 1) * width])
        out_ref[chunk] = part.astype(jnp.bfloat16)


def body(
    frames,
    lengths,
    norm_gain,
    qkv_weight,
    out_weight,
    conv_gain,
    glu_weight,
    conv_taps,
    point_weight,
):
    rows, model_width = frames.shape
    group_cols = qkv_weight.shape[2]
    chan_cols = glu_weight.shape[2]
    parts = lax.axis_size("tp")
    out_cols = model_width // parts
    bf16 = jnp.bfloat16
    qkv = jnp.swapaxes(qkv_weight, 0, 1)

    shape = jax.ShapeDtypeStruct

    query, keys_values = pl.pallas_call(
        project_kernel,
        in_specs=[HBM, HBM, HBM],
        out_specs=[VMEM, VMEM],
        out_shape=[shape((rows, group_cols), bf16), shape((rows, 2 * group_cols), bf16)],
        scratch_shapes=[
            pltpu.VMEM((rows, model_width), bf16),
            pltpu.VMEM((model_width // LANES, LANES), jnp.float32),
            pltpu.VMEM((3, model_width, group_cols), bf16),
            pltpu.VMEM((rows, model_width), bf16),
            pltpu.SemaphoreType.DMA((6,)),
        ],
        compiler_params=params(53),
        cost_estimate=cost(6 * rows * model_width * group_cols, 5_000_000),
        name="project",
    )(frames, norm_gain.reshape(-1, LANES), qkv)
    inner = swap_within_chip(keys_values)
    outer = swap_between_chips(keys_values)

    own_weights = pl.pallas_call(
        weigh_kernel,
        in_specs=[SMEM, VMEM, VMEM],
        out_specs=VMEM,
        out_shape=shape((group_cols // HEAD, rows, rows), jnp.float32),
        compiler_params=params(16),
        cost_estimate=cost(10**9, 2_000_000, 4 * rows * rows),
        name="weigh",
    )(lengths, query, keys_values)
    attn_terms = pl.pallas_call(
        attend_kernel,
        in_specs=[SMEM] + [VMEM] * 6,
        out_specs=VMEM,
        out_shape=shape((parts, rows, out_cols), bf16),
        compiler_params=params(16),
        cost_estimate=cost(10**9, 4_000_000, 4 * rows * rows),
        name="attend",
    )(lengths, query, own_weights, keys_values, inner, outer, out_weight)
    attn_terms = lax.all_to_all(attn_terms, "tp", 0, 0, tiled=True)
    own_frames = lax.dynamic_slice_in_dim(frames, lax.axis_index("tp") * out_cols, out_cols, 1)
    residual, rounded = pl.pallas_call(
        merge_kernel,
        in_specs=[VMEM] * 2,
        out_specs=[VMEM] * 2,
        out_shape=[shape((rows, out_cols), jnp.float32), shape((rows, out_cols), bf16)],
        compiler_params=params(16),
        cost_estimate=cost(10**6, 2_000_000),
        name="merge",
    )(attn_terms, own_frames)
    gathered = lax.all_gather(rounded, "tp", axis=0)
    gated, outer_rows, inner_rows = pl.pallas_call(
        glu_kernel,
        in_specs=[VMEM] * 3,
        out_specs=[VMEM] * 3,
        out_shape=[shape((rows, chan_cols), bf16)] + [shape((HALO, chan_cols), bf16)] * 2,
        compiler_params=params(),
        cost_estimate=cost(4 * rows * model_width * chan_cols, 3_500_000),
        name="glu",
    )(gathered, conv_gain.reshape(-1, LANES), jnp.swapaxes(glu_weight, 0, 1))
    outer_rows = swap_between_chips(outer_rows)
    inner_rows = swap_within_chip(inner_rows)
    inside = pl.pallas_call(
        inside_kernel,
        in_specs=[SMEM, VMEM, VMEM],
        out_specs=VMEM,
        out_shape=shape((rows - 2 * HALO, chan_cols), bf16),
        scratch_shapes=[
            pltpu.VMEM((rows, chan_cols), jnp.float32),
            pltpu.VMEM((8, rows - 3 * HALO // 2, chan_cols), jnp.float32),
        ],
        compiler_params=params(),
        cost_estimate=cost(10**9, 4_000_000),
        name="inside",
    )(lengths, gated, conv_taps)
    conv_terms = pl.pallas_call(
        conv_kernel,
        in_specs=[SMEM] + [VMEM] * 6,
        out_specs=VMEM,
        out_shape=shape((parts, rows, out_cols), bf16),
        scratch_shapes=[pltpu.VMEM((3 * HALO, chan_cols), jnp.float32)] * 2,
        compiler_params=params(),
        cost_estimate=cost(2 * rows * model_width * chan_cols, 2_500_000),
        name="conv",
    )(lengths, outer_rows, inner_rows, gated, inside, conv_taps, point_weight)
    conv_terms = lax.all_to_all(conv_terms, "tp", 0, 0, tiled=True)
    return pl.pallas_call(
        finish_kernel,
        in_specs=[VMEM] * 2,
        out_specs=VMEM,
        out_shape=shape((rows, out_cols), bf16),
        compiler_params=params(16),
        cost_estimate=cost(10**6, 2_000_000),
        name="finish",
    )(conv_terms, residual)


def solution(mesh):
    return jax.shard_map(
        body,
        mesh=mesh,
        in_specs=(
            P(("seq", "dp"), None),
            P(),
            P(),
            P(None, None, "tp"),
            P("tp", None),
            P(),
            P(None, None, "tp"),
            P(None, "tp"),
            P("tp", None),
        ),
        out_specs=P(("seq", "dp"), "tp"),
        check_vma=False,
    )
```
